32 devices in a mesh: row: 8 (over y, x, core), col: 4 (over z).
Axes of the slice: x: 2, y: 2, z: 4, core: 2. Of those that a mesh axis runs over, the one named last changes fastest.
Arguments:
- eigen_rows: float32 [1024, 65536], P(('col', 'row')), may hold values from -6 to 6
- householder: float32 [65536, 1024], P('row', 'col'), may hold values from -0.046875 to 0.046875
- owners: int32 [2], replicated, may hold values from 0 to 3, as said below
Outputs:
- vectors: float32 [1024, 65536], P('col', 'row')
The draws below stay inside these ranges and needn't reach their ends.
Inputs may be any that keep to these rules, and one draw needn't show every extreme that they name: `owners`: 2 distinct block indices below 4.
All inputs are finite; a program needn't handle non-finite values.
Results may differ from the reference program's by a relative error of at most 0.0001.
Values sent between devices are 32-bit elements; how exact they have to be, the bound alone decides.
A program may use at most 192 MiB of HBM per device.

```python
import jax
import jax.numpy as jnp
from jax import lax

N = 65536
M = 1024
B = 256
PANELS = 2
SLOTS = 1024
N_COL = 4


def draw_owners(key, part):
    key = jax.random.fold_in(key, 7)
    scores = jax.random.randint(key, (N_COL,), 0, 1 << 20, dtype=jnp.int32)
    scores = scores * N_COL + jnp.arange(N_COL, dtype=jnp.int32)
    order = jnp.argsort(scores, stable=True).astype(jnp.int32)
    return order[:PANELS].astype(jnp.int32)


def block_scale(stream_key, extent, shards, least, largest):
    loudness = 1.0
    for dim, shards_of in shards:
        steps = jax.random.uniform(jax.random.fold_in(jax.random.fold_in(stream_key, 6), dim), (shards_of,), jnp.float32, least / len(shards), largest / len(shards))
        loudness = loudness * jnp.repeat(jnp.exp(steps), extent[dim] // shards_of).reshape((-1,) + (1,) * (len(extent) - 1 - dim))
    return loudness


def gaussian(stream_key, dims, deviation, limit, shards=(), held_as=jnp.bfloat16):
    loudness = block_scale(stream_key, dims, shards, -0.22, 0.18) if shards else 1.0
    values = jax.random.normal(stream_key, dims, jnp.float32) * deviation * loudness
    return jnp.minimum(jnp.maximum(values, -limit), limit).astype(held_as)


def setup_inputs(seed: int = 0) -> dict:
    key_of = jax.random.split(jax.random.key(seed), 4)
    eigen_rows = gaussian(key_of[0], (M, N), 1.0, 6.0, ((0, 32),), jnp.float32)
    householder = gaussian(key_of[1], (N, SLOTS), (N // 4) ** -0.5, 0.046875, ((0, 8), (1, 4)), jnp.float32)
    owners = draw_owners(jax.random.fold_in(key_of[3], 71), 0)
    return {"eigen_rows": eigen_rows, "householder": householder, "owners": owners}


def shape_panel(stored, first_row, offset):
    rows = first_row + lax.broadcasted_iota(jnp.int32, stored.shape, 0)
    cols = offset + lax.broadcasted_iota(jnp.int32, stored.shape, 1)
    unit = jnp.where(rows == cols, jnp.ones_like(stored), jnp.zeros_like(stored))
    return jnp.where(rows > cols, stored, unit)


def matmul_full(left, right):
    return jnp.dot(left, right, precision=lax.Precision.HIGHEST)


def inverse_factor(gram):
    width = gram.shape[0]
    rows = lax.broadcasted_iota(jnp.int32, gram.shape, 0)
    cols = lax.broadcasted_iota(jnp.int32, gram.shape, 1)
    ident = jnp.where(rows == cols, jnp.ones_like(gram), jnp.zeros_like(gram))
    half_diag = jnp.sum(gram * ident, axis=1) * 0.5
    strict = jnp.where(cols > rows, gram, jnp.zeros_like(gram)) / half_diag[:, None]
    result = ident - strict
    power = strict
    reach = 2
    while reach < width:
        power = matmul_full(power, power)
        result = matmul_full(result, ident + power)
        reach = reach * 2
    return result / half_diag[None, :]


def reflect(current, panel):
    gram = lax.dot_general(panel, panel, (((0,), (0,)), ((), ())), precision=lax.Precision.HIGHEST)
    inner = jnp.dot(current, panel, precision=lax.Precision.HIGHEST)
    inverse = inverse_factor(gram)
    solved = lax.dot_general(inner, inverse, (((1,), (1,)), ((), ())), precision=lax.Precision.HIGHEST)
    update = lax.dot_general(solved, panel, (((1,), (1,)), ((), ())), precision=lax.Precision.HIGHEST)
    return current - update


def reference(eigen_rows, householder, owners):
    current = eigen_rows
    for panel_index in reversed(range(PANELS)):
        start = (owners[panel_index] * B).astype(jnp.int32)
        stored = lax.dynamic_slice_in_dim(householder, start, B, 1)
        panel = shape_panel(stored, 0, panel_index * B)
        current = reflect(current, panel)
    return current
```

```python
import functools

import jax
import jax.numpy as jnp
from jax import lax
from jax.experimental import pallas as pl
from jax.experimental.pallas import tpu as pltpu
from jax.sharding import PartitionSpec as P

PANELS = 2
MESH = pl.DeviceIdType.MESH
FULL = lax.Precision.HIGHEST


def dot(left, right, left_dim=1, right_dim=0):
    return lax.dot_general(
        left, right, (((left_dim,), (right_dim,)), ((), ())),
        precision=FULL, preferred_element_type=jnp.float32,
    )


def inverse_factor(gram):
    width = gram.shape[0]
    rows = lax.broadcasted_iota(jnp.int32, gram.shape, 0)
    cols = lax.broadcasted_iota(jnp.int32, gram.shape, 1)
    ident = jnp.where(rows == cols, 1.0, 0.0)
    half_down = jnp.sum(gram * ident, axis=1, keepdims=True) * 0.5
    half_across = jnp.sum(gram * ident, axis=0, keepdims=True) * 0.5
    strict = jnp.where(cols > rows, gram, 0.0) / half_down
    result = ident - strict
    power = strict
    reach = 2
    while reach < width:
        power = dot(power, power)
        result = dot(result, ident + power)
        reach = reach * 2
    return result / half_across


def kernel(
    row_n, col_n, chunk, exchange, eigen_ref, house_ref, flag_ref, out_ref,
    right_buf, left_buf, own, current, acc, parts, full, solved,
    right_send, right_recv, left_send, left_recv,
    swap_send, swap_recv, part_send, part_recv, full_send, full_recv, own_sem, here_sem, out_sem,
):
    row = lax.axis_index("row")
    col = lax.axis_index("col")
    row_count, width = own.shape
    mine_rows = current.shape[0]
    per_panel = row_count // chunk
    total = PANELS * per_panel
    share = parts.shape[1]
    grams = PANELS + 1

    own_copy = pltpu.make_async_copy(house_ref, own, own_sem)
    own_copy.start()
    if exchange:
        give = eigen_ref.shape[0]
        here = pltpu.make_async_copy(
            eigen_ref.at[:, pl.ds(pl.multiple_of(row * row_count, 128), row_count)],
            current.at[pl.ds(pl.multiple_of(row * give, 8), give), :], here_sem,
        )
    else:
        here = pltpu.make_async_copy(eigen_ref, current, here_sem)
    here.start()

    barrier = pltpu.get_barrier_semaphore()
    for step in range(1, row_n):
        pl.semaphore_signal(
            barrier, inc=1, device_id=(lax.rem(row + step, row_n), col), device_id_type=MESH)

    @pl.when(col > 0)
    def _():
        pl.semaphore_signal(barrier, inc=1, device_id=(row, col - 1), device_id_type=MESH)

    @pl.when(col < col_n - 1)
    def _():
        pl.semaphore_signal(barrier, inc=1, device_id=(row, col + 1), device_id_type=MESH)

    beside = jnp.where(col > 0, 1, 0) + jnp.where(col < col_n - 1, 1, 0)
    pl.semaphore_wait(barrier, row_n - 1 + beside)

    def swap(step):
        peer = lax.rem(row + step, row_n)
        return pltpu.make_async_remote_copy(
            src_ref=eigen_ref.at[:, pl.ds(pl.multiple_of(peer * row_count, 128), row_count)],
            dst_ref=current.at[pl.ds(pl.multiple_of(row * give, 8), give), :],
            send_sem=swap_send.at[step], recv_sem=swap_recv.at[step],
            device_id=(peer, col), device_id_type=MESH,
        )

    if exchange:
        for step in range(1, row_n):
            swap(step).start()
    own_copy.wait()

    def piece(index):
        return pl.ds(pl.multiple_of(index * chunk, chunk), chunk)

    def to_right(index):
        at = piece(index)
        return pltpu.make_async_remote_copy(
            src_ref=right_buf.at[at, :], dst_ref=right_buf.at[at, :],
            send_sem=right_send.at[index], recv_sem=right_recv.at[index],
            device_id=(row, lax.rem(col + 1, col_n)), device_id_type=MESH,
        )

    def to_left(index):
        at = piece(index)
        return pltpu.make_async_remote_copy(
            src_ref=left_buf.at[at, :], dst_ref=left_buf.at[at, :],
            send_sem=left_send.at[index], recv_sem=left_recv.at[index],
            device_id=(row, lax.rem(col + col_n - 1, col_n)), device_id_type=MESH,
        )

    def flag(index):
        return jnp.broadcast_to(flag_ref[pl.ds(index, 1), :], (chunk, width)) > 0

    def pass_on(index, buf, copy, first, last):
        at = piece(index)
        panel = index // per_panel
        stored = own[piece(lax.rem(index, per_panel)), :]

        @pl.when(first)
        def _():
            buf[at, :] = stored

        @pl.when(jnp.logical_not(first))
        def _():
            copy(index).wait_recv()
            buf[at, :] = jnp.where(flag(panel), stored, buf[at, :])

        @pl.when(jnp.logical_not(last))
        def _():
            copy(index).start()

    def reflectors(panel, block):
        at = piece(panel * per_panel + block)
        stored = jnp.where(flag(PANELS + panel), right_buf[at, :], left_buf[at, :])
        rows = row * row_count + block * chunk + lax.broadcasted_iota(jnp.int32, stored.shape, 0)
        cols = (PANELS - 1 - panel) * width + lax.broadcasted_iota(jnp.int32, stored.shape, 1)
        return jnp.where(rows > cols, stored, jnp.where(rows == cols, 1.0, 0.0))

    def add(start, size, value):
        acc[start:start + size, :] = acc[start:start + size, :] + value

    acc[...] = jnp.zeros_like(acc)
    from_left = col
    from_right = col_n - 1 - col

    @pl.loop(0, total + 2 * (col_n - 1))
    def _(step):
        index_right = step - 2 * from_left

        @pl.when(jnp.logical_and(index_right >= 0, index_right < total))
        def _():
            pass_on(index_right, right_buf, to_right, col == 0, col == col_n - 1)

        index_left = step - 2 * from_right

        @pl.when(jnp.logical_and(index_left >= 0, index_left < total))
        def _():
            pass_on(index_left, left_buf, to_left, col == col_n - 1, col == 0)

        index = step - 2 * jnp.maximum(from_left, from_right)

        @pl.when(jnp.logical_and(index >= 0, index < per_panel))
        def _():
            panel = reflectors(0, index)
            add(0, width, dot(panel, panel, 0, 0))

        @pl.when(index == per_panel)
        def _():
            here.wait()
            if exchange:
                for other in range(1, row_n):
                    swap(other).wait_recv()

        @pl.when(jnp.logical_and(index >= per_panel, index < total))
        def _():
            block = index - per_panel
            first = reflectors(0, block)
            second = reflectors(1, block)
            held = current[:, piece(block)]
            add(width, width, dot(second, second, 0, 0))
            add(2 * width, width, dot(first, second, 0, 0))
            add(grams * width, mine_rows, dot(held, first))
            add(grams * width + mine_rows, mine_rows, dot(held, second))

    def part(index):
        return pl.ds(pl.multiple_of(index * share, 8), share)

    def part_copy(step):
        peer = lax.rem(row + step, row_n)
        return pltpu.make_async_remote_copy(
            src_ref=acc.at[part(peer), :], dst_ref=parts.at[step],
            send_sem=part_send.at[step], recv_sem=part_recv.at[step],
            device_id=(peer, col), device_id_type=MESH,
        )

    def full_copy(step):
        return pltpu.make_async_remote_copy(
            src_ref=full.at[part(row), :], dst_ref=full.at[part(row), :],
            send_sem=full_send.at[step], recv_sem=full_recv.at[step],
            device_id=(lax.rem(row + step, row_n), col), device_id_type=MESH,
        )

    for step in range(1, row_n):
        part_copy(step).start()
    summed = acc[part(row), :]
    for step in range(1, row_n):
        part_copy(step).wait_recv()
        summed = summed + parts[step]
    full[part(row), :] = summed
    for step in range(1, row_n):
        full_copy(step).start()
    for step in range(1, row_n):
        full_copy(step).wait_recv()

    inner = grams * width
    inverse_first = inverse_factor(full[0:width, :])
    inverse_second = inverse_factor(full[width:2 * width, :])
    solved_first = dot(full[inner:inner + mine_rows, :], inverse_first, 1, 1)
    inner_second = full[inner + mine_rows:inner + 2 * mine_rows, :] - dot(
        solved_first, full[2 * width:3 * width, :])
    solved[0] = solved_first
    solved[1] = dot(inner_second, inverse_second, 1, 1)

    def out_copy(block):
        at = piece(block)
        return pltpu.make_async_copy(current.at[:, at], out_ref.at[:, at], out_sem.at[block])

    @pl.loop(0, per_panel)
    def _(block):
        update = dot(solved[0], reflectors(0, block), 1, 1) + dot(
            solved[1], reflectors(1, block), 1, 1)
        at = piece(block)
        current[:, at] = current[:, at] - update
        out_copy(block).start()

    @pl.loop(0, total)
    def _(index):
        @pl.when(col < col_n - 1)
        def _():
            to_right(index).wait_send()

        @pl.when(col > 0)
        def _():
            to_left(index).wait_send()

    for step in range(1, row_n):
        if exchange:
            swap(step).wait_send()
        part_copy(step).wait_send()
        full_copy(step).wait_send()

    @pl.loop(0, per_panel)
    def _(block):
        out_copy(block).wait()


def on_device(row_n, col_n, eigen_rows, householder, owners):
    row_count, width = householder.shape
    give = eigen_rows.shape[0]
    mine_rows = give * row_n
    exchange = give % 8 == 0
    if not exchange:
        eigen_rows = lax.all_to_all(eigen_rows, "row", split_axis=1, concat_axis=0, tiled=True)
    chunk = min(256, row_count)
    per_panel = row_count // chunk
    total = PANELS * per_panel
    col = lax.axis_index("col")
    order = owners[::-1]
    flags = jnp.concatenate([order == col, order <= col]).astype(jnp.int32)
    flags = jnp.broadcast_to(
        jnp.pad(flags, (0, 8 - 2 * PANELS))[:, None], (8, width))
    rows = (PANELS + 1) * width + PANELS * mine_rows
    share = -(-rows // (8 * row_n)) * 8
    dma = pltpu.SemaphoreType.DMA
    return pl.pallas_call(
        functools.partial(kernel, row_n, col_n, chunk, exchange),
        out_shape=jax.ShapeDtypeStruct((mine_rows, row_count), jnp.float32),
        in_specs=[
            pl.BlockSpec(memory_space=pl.ANY),
            pl.BlockSpec(memory_space=pl.ANY),
            pl.BlockSpec(memory_space=pltpu.VMEM),
        ],
        out_specs=pl.BlockSpec(memory_space=pl.ANY),
        scratch_shapes=[
            pltpu.VMEM((PANELS * row_count, width), jnp.float32),
            pltpu.VMEM((PANELS * row_count, width), jnp.float32),
            pltpu.VMEM((row_count, width), jnp.float32),
            pltpu.VMEM((mine_rows, row_count), jnp.float32),
            pltpu.VMEM((share * row_n, width), jnp.float32),
            pltpu.VMEM((row_n, share, width), jnp.float32),
            pltpu.VMEM((share * row_n, width), jnp.float32),
            pltpu.VMEM((PANELS, mine_rows, width), jnp.float32),
            dma((total,)), dma((total,)), dma((total,)), dma((total,)),
            dma((row_n,)), dma((row_n,)), dma((row_n,)), dma((row_n,)),
            dma((row_n,)), dma((row_n,)),
            dma, dma, dma((per_panel,)),
        ],
        compiler_params=pltpu.CompilerParams(
            collective_id=0, has_side_effects=True, vmem_limit_bytes=60 * 2**20),
    )(eigen_rows, householder, flags)


def solution(mesh):
    return jax.shard_map(
        functools.partial(on_device, mesh.shape["row"], mesh.shape["col"]),
        mesh=mesh,
        in_specs=(P(("col", "row"), None), P("row", "col"), P()),
        out_specs=P("col", "row"),
        check_vma=False,
    )
```

```python
import functools

import jax
import jax.numpy as jnp
from jax import lax
from jax.experimental import pallas as pl
from jax.experimental.pallas import tpu as pltpu
from jax.sharding import PartitionSpec as P

PANELS = 2
MESH = pl.DeviceIdType.MESH
FULL = lax.Precision.HIGHEST


def dot(left, right, left_dim=1, right_dim=0):
    return lax.dot_general(
        left, right, (((left_dim,), (right_dim,)), ((), ())),
        precision=FULL, preferred_element_type=jnp.float32,
    )


def halves(value):
    high = value.astype(jnp.bfloat16)
    return high, (value - high.astype(jnp.float32)).astype(jnp.bfloat16)


def dot_halves(left, right, left_dim=1, right_dim=0):
    def one(a, b):
        return lax.dot_general(
            a, b, (((left_dim,), (right_dim,)), ((), ())), preferred_element_type=jnp.float32)

    return one(left[0], right[0]) + (one(left[0], right[1]) + one(left[1], right[0]))


def dot_split(left, right, left_dim=1, right_dim=0):
    return dot_halves(halves(left), halves(right), left_dim, right_dim)


def inverse_factor(gram):
    width = gram.shape[0]
    rows = lax.broadcasted_iota(jnp.int32, gram.shape, 0)
    cols = lax.broadcasted_iota(jnp.int32, gram.shape, 1)
    ident = jnp.where(rows == cols, 1.0, 0.0)
    half_down = jnp.sum(gram * ident, axis=1, keepdims=True) * 0.5
    half_across = jnp.sum(gram * ident, axis=0, keepdims=True) * 0.5
    strict = jnp.where(cols > rows, gram, 0.0) / half_down
    result = ident - strict
    power = strict
    reach = 2
    while reach < width:
        power = dot_split(power, power)
        result = result + dot_split(result, power)
        reach = reach * 2
    return result / half_across


def kernel(
    row_n, col_n, chunk, exchange, eigen_ref, house_ref, flag_ref, out_ref,
    right_buf, left_buf, own, current, acc, parts, full, solved,
    right_send, right_recv, left_send, left_recv,
    swap_send, swap_recv, part_send, part_recv, full_send, full_recv, own_sem, here_sem, out_sem,
):
    row = lax.axis_index("row")
    col = lax.axis_index("col")
    row_count, width = own.shape
    mine_rows = current.shape[0]
    per_panel = row_count // chunk
    total = PANELS * per_panel
    share = parts.shape[2]

    own_copy = pltpu.make_async_copy(house_ref, own, own_sem)
    own_copy.start()
    if exchange:
        give = eigen_ref.shape[0]
        here = pltpu.make_async_copy(
            eigen_ref.at[:, pl.ds(pl.multiple_of(row * row_count, 128), row_count)],
            current.at[pl.ds(pl.multiple_of(row * give, 8), give), :], here_sem,
        )
    else:
        here = pltpu.make_async_copy(eigen_ref, current, here_sem)
    here.start()

    barrier = pltpu.get_barrier_semaphore()
    for step in range(1, row_n):
        pl.semaphore_signal(
            barrier, inc=1, device_id=(lax.rem(row + step, row_n), col), device_id_type=MESH)

    @pl.when(col > 0)
    def _():
        pl.semaphore_signal(barrier, inc=1, device_id=(row, col - 1), device_id_type=MESH)

    @pl.when(col < col_n - 1)
    def _():
        pl.semaphore_signal(barrier, inc=1, device_id=(row, col + 1), device_id_type=MESH)

    beside = jnp.where(col > 0, 1, 0) + jnp.where(col < col_n - 1, 1, 0)
    pl.semaphore_wait(barrier, row_n - 1 + beside)

    def swap(step):
        peer = lax.rem(row + step, row_n)
        return pltpu.make_async_remote_copy(
            src_ref=eigen_ref.at[:, pl.ds(pl.multiple_of(peer * row_count, 128), row_count)],
            dst_ref=current.at[pl.ds(pl.multiple_of(row * give, 8), give), :],
            send_sem=swap_send.at[step], recv_sem=swap_recv.at[step],
            device_id=(peer, col), device_id_type=MESH,
        )

    if exchange:
        for step in range(1, row_n):
            swap(step).start()
    own_copy.wait()

    def piece(index):
        return pl.ds(pl.multiple_of(index * chunk, chunk), chunk)

    def to_right(index):
        at = piece(index)
        return pltpu.make_async_remote_copy(
            src_ref=right_buf.at[at, :], dst_ref=right_buf.at[at, :],
            send_sem=right_send.at[index], recv_sem=right_recv.at[index],
            device_id=(row, lax.rem(col + 1, col_n)), device_id_type=MESH,
        )

    def to_left(index):
        at = piece(index)
        return pltpu.make_async_remote_copy(
            src_ref=left_buf.at[at, :], dst_ref=left_buf.at[at, :],
            send_sem=left_send.at[index], recv_sem=left_recv.at[index],
            device_id=(row, lax.rem(col + col_n - 1, col_n)), device_id_type=MESH,
        )

    def flag(index):
        return jnp.broadcast_to(flag_ref[pl.ds(index, 1), :], (chunk, width)) > 0

    def pass_on(index, buf, copy, first, last):
        at = piece(index)
        panel = index // per_panel
        stored = own[piece(lax.rem(index, per_panel)), :]

        @pl.when(first)
        def _():
            buf[at, :] = stored

        @pl.when(jnp.logical_not(first))
        def _():
            copy(index).wait_recv()
            buf[at, :] = jnp.where(flag(panel), stored, buf[at, :])

        @pl.when(jnp.logical_not(last))
        def _():
            copy(index).start()

    def reflectors(panel, block):
        at = piece(panel * per_panel + block)
        stored = jnp.where(flag(PANELS + panel), right_buf[at, :], left_buf[at, :])
        rows = row * row_count + block * chunk + lax.broadcasted_iota(jnp.int32, stored.shape, 0)
        cols = (PANELS - 1 - panel) * width + lax.broadcasted_iota(jnp.int32, stored.shape, 1)
        return jnp.where(rows > cols, stored, jnp.where(rows == cols, 1.0, 0.0))

    def add(panel, start, size, value):
        acc[panel, start:start + size, :] = acc[panel, start:start + size, :] + value

    def add_inner(panel, block):
        add(panel, width, mine_rows, dot(current[:, piece(block)], reflectors(panel, block)))

    def part(index):
        return pl.ds(pl.multiple_of(index * share, 8), share)

    def part_copy(panel, step):
        peer = lax.rem(row + step, row_n)
        return pltpu.make_async_remote_copy(
            src_ref=acc.at[panel, part(peer), :], dst_ref=parts.at[panel, step],
            send_sem=part_send.at[panel, step], recv_sem=part_recv.at[panel, step],
            device_id=(peer, col), device_id_type=MESH,
        )

    def full_copy(panel, step):
        return pltpu.make_async_remote_copy(
            src_ref=full.at[panel, part(row), :], dst_ref=full.at[panel, part(row), :],
            send_sem=full_send.at[panel, step], recv_sem=full_recv.at[panel, step],
            device_id=(lax.rem(row + step, row_n), col), device_id_type=MESH,
        )

    def give_parts(panel):
        for step in range(1, row_n):
            part_copy(panel, step).start()

    def give_sums(panel):
        summed = acc[panel, part(row), :]
        for step in range(1, row_n):
            part_copy(panel, step).wait_recv()
            summed = summed + parts[panel, step]
        full[panel, part(row), :] = summed
        for step in range(1, row_n):
            full_copy(panel, step).start()

    def solve(panel):
        for step in range(1, row_n):
            full_copy(panel, step).wait_recv()
        inverse = inverse_factor(full[panel, 0:width, :])
        solved[panel] = dot_split(full[panel, width:width + mine_rows, :], inverse, 1, 1)

    acc[...] = jnp.zeros_like(acc)
    from_left = col
    from_right = col_n - 1 - col
    late = per_panel - per_panel // 4

    @pl.loop(0, total + 2 * (col_n - 1))
    def _(step):
        index_right = step - 2 * from_left

        @pl.when(jnp.logical_and(index_right >= 0, index_right < total))
        def _():
            pass_on(index_right, right_buf, to_right, col == 0, col == col_n - 1)

        index_left = step - 2 * from_right

        @pl.when(jnp.logical_and(index_left >= 0, index_left < total))
        def _():
            pass_on(index_left, left_buf, to_left, col == col_n - 1, col == 0)

        index = step - 2 * jnp.maximum(from_left, from_right)

        @pl.when(jnp.logical_and(index >= 0, index < per_panel))
        def _():
            panel = reflectors(0, index)
            add(0, 0, width, dot(panel, panel, 0, 0))

        @pl.when(index == late)
        def _():
            here.wait()
            if exchange:
                for other in range(1, row_n):
                    swap(other).wait_recv()

        @pl.when(jnp.logical_and(index >= late, index < per_panel))
        def _():
            @pl.loop(0, 4)
            def _(more):
                add_inner(0, (index - late) * 4 + more)

        block = index - per_panel

        @pl.when(block == 0)
        def _():
            give_parts(0)

        @pl.when(block == per_panel // 8)
        def _():
            give_sums(0)

        @pl.when(block == per_panel // 4 - 1)
        def _():
            solve(0)

        @pl.when(jnp.logical_and(block >= 0, block < per_panel))
        def _():
            panel = reflectors(1, block)
            add(1, 0, width, dot(panel, panel, 0, 0))

        @pl.when(jnp.logical_and(block >= per_panel // 4, block < per_panel // 2))
        def _():
            @pl.loop(0, 4)
            def _(more):
                other = (block - per_panel // 4) * 4 + more
                at = piece(other)
                current[:, at] = current[:, at] - dot(solved[0], reflectors(0, other), 1, 1)

        @pl.when(jnp.logical_and(block >= per_panel // 2, block < per_panel))
        def _():
            for more in range(2):
                add_inner(1, (block - per_panel // 2) * 2 + more)

    give_parts(1)
    give_sums(1)
    solve(1)

    def out_copy(block):
        at = piece(block)
        return pltpu.make_async_copy(current.at[:, at], out_ref.at[:, at], out_sem.at[block])

    @pl.loop(0, per_panel)
    def _(block):
        update = dot_halves(halves(solved[1]), halves(reflectors(1, block)), 1, 1)
        at = piece(block)
        current[:, at] = current[:, at] - update
        out_copy(block).start()

    @pl.loop(0, total)
    def _(index):
        @pl.when(col < col_n - 1)
        def _():
            to_right(index).wait_send()

        @pl.when(col > 0)
        def _():
            to_left(index).wait_send()

    for step in range(1, row_n):
        if exchange:
            swap(step).wait_send()
        for panel in range(PANELS):
            part_copy(panel, step).wait_send()
            full_copy(panel, step).wait_send()

    @pl.loop(0, per_panel)
    def _(block):
        out_copy(block).wait()


def on_device(row_n, col_n, eigen_rows, householder, owners):
    row_count, width = householder.shape
    give = eigen_rows.shape[0]
    mine_rows = give * row_n
    exchange = give % 8 == 0
    if not exchange:
        eigen_rows = lax.all_to_all(eigen_rows, "row", split_axis=1, concat_axis=0, tiled=True)
    chunk = min(256, row_count)
    per_panel = row_count // chunk
    total = PANELS * per_panel
    col = lax.axis_index("col")
    order = owners[::-1]
    flags = jnp.concatenate([order == col, order <= col]).astype(jnp.int32)
    flags = jnp.broadcast_to(
        jnp.pad(flags, (0, 8 - 2 * PANELS))[:, None], (8, width))
    rows = width + mine_rows
    share = -(-rows // (8 * row_n)) * 8
    dma = pltpu.SemaphoreType.DMA
    return pl.pallas_call(
        functools.partial(kernel, row_n, col_n, chunk, exchange),
        out_shape=jax.ShapeDtypeStruct((mine_rows, row_count), jnp.float32),
        in_specs=[
            pl.BlockSpec(memory_space=pl.ANY),
            pl.BlockSpec(memory_space=pl.ANY),
            pl.BlockSpec(memory_space=pltpu.VMEM),
        ],
        out_specs=pl.BlockSpec(memory_space=pl.ANY),
        scratch_shapes=[
            pltpu.VMEM((PANELS * row_count, width), jnp.float32),
            pltpu.VMEM((PANELS * row_count, width), jnp.float32),
            pltpu.VMEM((row_count, width), jnp.float32),
            pltpu.VMEM((mine_rows, row_count), jnp.float32),
            pltpu.VMEM((PANELS, share * row_n, width), jnp.float32),
            pltpu.VMEM((PANELS, row_n, share, width), jnp.float32),
            pltpu.VMEM((PANELS, share * row_n, width), jnp.float32),
            pltpu.VMEM((PANELS, mine_rows, width), jnp.float32),
            dma((total,)), dma((total,)), dma((total,)), dma((total,)),
            dma((row_n,)), dma((row_n,)),
            dma((PANELS, row_n)), dma((PANELS, row_n)),
            dma((PANELS, row_n)), dma((PANELS, row_n)),
            dma, dma, dma((per_panel,)),
        ],
        compiler_params=pltpu.CompilerParams(
            collective_id=0, has_side_effects=True, vmem_limit_bytes=60 * 2**20),
    )(eigen_rows, householder, flags)


def solution(mesh):
    return jax.shard_map(
        functools.partial(on_device, mesh.shape["row"], mesh.shape["col"]),
        mesh=mesh,
        in_specs=(P(("col", "row"), None), P("row", "col"), P()),
        out_specs=P("col", "row"),
        check_vma=False,
    )
```

```python
import functools

import jax
import jax.numpy as jnp
from jax import lax
from jax.experimental import pallas as pl
from jax.experimental.pallas import tpu as pltpu
from jax.sharding import PartitionSpec as P

PANELS = 2
MESH = pl.DeviceIdType.MESH
FULL = lax.Precision.HIGHEST


def dot(left, right, left_dim=1, right_dim=0):
    return lax.dot_general(
        left, right, (((left_dim,), (right_dim,)), ((), ())),
        precision=FULL, preferred_element_type=jnp.float32,
    )


def halves(value):
    high = value.astype(jnp.bfloat16)
    return high, (value - high.astype(jnp.float32)).astype(jnp.bfloat16)


def dot_halves(left, right, left_dim=1, right_dim=0):
    def one(a, b):
        return lax.dot_general(
            a, b, (((left_dim,), (right_dim,)), ((), ())), preferred_element_type=jnp.float32)

    return one(left[0], right[0]) + (one(left[0], right[1]) + one(left[1], right[0]))


def dot_split(left, right, left_dim=1, right_dim=0):
    return dot_halves(halves(left), halves(right), left_dim, right_dim)


def inverse_factor(gram):
    width = gram.shape[0]
    rows = lax.broadcasted_iota(jnp.int32, gram.shape, 0)
    cols = lax.broadcasted_iota(jnp.int32, gram.shape, 1)
    ident = jnp.where(rows == cols, 1.0, 0.0)
    half_down = jnp.sum(gram * ident, axis=1, keepdims=True) * 0.5
    half_across = jnp.sum(gram * ident, axis=0, keepdims=True) * 0.5
    strict = jnp.where(cols > rows, gram, 0.0) / half_down
    result = ident - strict
    power = strict
    reach = 2
    while reach < width:
        power = dot_split(power, power)
        result = result + dot_split(result, power)
        reach = reach * 2
    return result / half_across


def kernel(
    row_n, col_n, chunk, exchange, eigen_ref, house_ref, flag_ref, held_ref, panel_ref, solved_ref,
    right_buf, left_buf, own, current, acc, parts, full, solved,
    right_send, right_recv, left_send, left_recv,
    swap_send, swap_recv, part_send, part_recv, full_send, full_recv, own_sem, here_sem, held_sem, panel_sem, solved_sem,
):
    row = lax.axis_index("row")
    col = lax.axis_index("col")
    row_count, width = own.shape
    mine_rows = current.shape[0]
    per_panel = row_count // chunk
    total = PANELS * per_panel
    share = parts.shape[2]

    own_copy = pltpu.make_async_copy(house_ref, own, own_sem)
    own_copy.start()
    if exchange:
        give = eigen_ref.shape[0]
        here = pltpu.make_async_copy(
            eigen_ref.at[:, pl.ds(pl.multiple_of(row * row_count, 128), row_count)],
            current.at[pl.ds(pl.multiple_of(row * give, 8), give), :], here_sem,
        )
    else:
        here = pltpu.make_async_copy(eigen_ref, current, here_sem)
    here.start()

    barrier = pltpu.get_barrier_semaphore()
    for step in range(1, row_n):
        pl.semaphore_signal(
            barrier, inc=1, device_id=(lax.rem(row + step, row_n), col), device_id_type=MESH)

    @pl.when(col > 0)
    def _():
        pl.semaphore_signal(barrier, inc=1, device_id=(row, col - 1), device_id_type=MESH)

    @pl.when(col < col_n - 1)
    def _():
        pl.semaphore_signal(barrier, inc=1, device_id=(row, col + 1), device_id_type=MESH)

    beside = jnp.where(col > 0, 1, 0) + jnp.where(col < col_n - 1, 1, 0)
    pl.semaphore_wait(barrier, row_n - 1 + beside)

    def swap(step):
        peer = lax.rem(row + step, row_n)
        return pltpu.make_async_remote_copy(
            src_ref=eigen_ref.at[:, pl.ds(pl.multiple_of(peer * row_count, 128), row_count)],
            dst_ref=current.at[pl.ds(pl.multiple_of(row * give, 8), give), :],
            send_sem=swap_send.at[step], recv_sem=swap_recv.at[step],
            device_id=(peer, col), device_id_type=MESH,
        )

    if exchange:
        for step in range(1, row_n):
            swap(step).start()
    own_copy.wait()

    def piece(index):
        return pl.ds(pl.multiple_of(index * chunk, chunk), chunk)

    def to_right(index):
        at = piece(index)
        return pltpu.make_async_remote_copy(
            src_ref=right_buf.at[at, :], dst_ref=right_buf.at[at, :],
            send_sem=right_send.at[index], recv_sem=right_recv.at[index],
            device_id=(row, lax.rem(col + 1, col_n)), device_id_type=MESH,
        )

    def to_left(index):
        at = piece(index)
        return pltpu.make_async_remote_copy(
            src_ref=left_buf.at[at, :], dst_ref=left_buf.at[at, :],
            send_sem=left_send.at[index], recv_sem=left_recv.at[index],
            device_id=(row, lax.rem(col + col_n - 1, col_n)), device_id_type=MESH,
        )

    def flag(index):
        return jnp.broadcast_to(flag_ref[pl.ds(index, 1), :], (chunk, width)) > 0

    def pass_on(index, buf, copy, first, last):
        at = piece(index)
        panel = index // per_panel
        stored = own[piece(lax.rem(index, per_panel)), :]

        @pl.when(first)
        def _():
            buf[at, :] = stored

        @pl.when(jnp.logical_not(first))
        def _():
            copy(index).wait_recv()
            buf[at, :] = jnp.where(flag(panel), stored, buf[at, :])

        @pl.when(jnp.logical_not(last))
        def _():
            copy(index).start()

    def reflectors(panel, block):
        at = piece(panel * per_panel + block)
        stored = jnp.where(flag(PANELS + panel), right_buf[at, :], left_buf[at, :])
        rows = row * row_count + block * chunk + lax.broadcasted_iota(jnp.int32, stored.shape, 0)
        cols = (PANELS - 1 - panel) * width + lax.broadcasted_iota(jnp.int32, stored.shape, 1)
        return jnp.where(rows > cols, stored, jnp.where(rows == cols, 1.0, 0.0))

    def held_copy(block):
        at = piece(block)
        return pltpu.make_async_copy(current.at[:, at], held_ref.at[:, at], held_sem.at[block])

    def panel_copy(block):
        at = piece(block)
        return pltpu.make_async_copy(own.at[at, :], panel_ref.at[at, :], panel_sem.at[block])

    def add(panel, start, size, value):
        acc[panel, start:start + size, :] = acc[panel, start:start + size, :] + value

    def add_inner(panel, block):
        add(panel, width, mine_rows, dot(current[:, piece(block)], reflectors(panel, block)))

    def part(index):
        return pl.ds(pl.multiple_of(index * share, 8), share)

    def part_copy(panel, step):
        peer = lax.rem(row + step, row_n)
        return pltpu.make_async_remote_copy(
            src_ref=acc.at[panel, part(peer), :], dst_ref=parts.at[panel, step],
            send_sem=part_send.at[panel, step], recv_sem=part_recv.at[panel, step],
            device_id=(peer, col), device_id_type=MESH,
        )

    def full_copy(panel, step):
        return pltpu.make_async_remote_copy(
            src_ref=full.at[panel, part(row), :], dst_ref=full.at[panel, part(row), :],
            send_sem=full_send.at[panel, step], recv_sem=full_recv.at[panel, step],
            device_id=(lax.rem(row + step, row_n), col), device_id_type=MESH,
        )

    def give_parts(panel):
        for step in range(1, row_n):
            part_copy(panel, step).start()

    def give_sums(panel):
        summed = acc[panel, part(row), :]
        for step in range(1, row_n):
            part_copy(panel, step).wait_recv()
            summed = summed + parts[panel, step]
        full[panel, part(row), :] = summed
        for step in range(1, row_n):
            full_copy(panel, step).start()

    def solve(panel):
        for step in range(1, row_n):
            full_copy(panel, step).wait_recv()
        inverse = inverse_factor(full[panel, 0:width, :])
        solved[panel] = dot_split(full[panel, width:width + mine_rows, :], inverse, 1, 1)

    acc[...] = jnp.zeros_like(acc)
    from_left = col
    from_right = col_n - 1 - col
    late = per_panel - per_panel // 4

    @pl.loop(0, total + 2 * (col_n - 1))
    def _(step):
        index_right = step - 2 * from_left

        @pl.when(jnp.logical_and(index_right >= 0, index_right < total))
        def _():
            pass_on(index_right, right_buf, to_right, col == 0, col == col_n - 1)

        index_left = step - 2 * from_right

        @pl.when(jnp.logical_and(index_left >= 0, index_left < total))
        def _():
            pass_on(index_left, left_buf, to_left, col == col_n - 1, col == 0)

        index = step - 2 * jnp.maximum(from_left, from_right)

        @pl.when(jnp.logical_and(index >= 0, index < per_panel))
        def _():
            panel = reflectors(0, index)
            add(0, 0, width, dot(panel, panel, 0, 0))

        @pl.when(index == late)
        def _():
            here.wait()
            if exchange:
                for other in range(1, row_n):
                    swap(other).wait_recv()

        @pl.when(jnp.logical_and(index >= late, index < per_panel))
        def _():
            @pl.loop(0, 4)
            def _(more):
                add_inner(0, (index - late) * 4 + more)

        block = index - per_panel

        @pl.when(block == 0)
        def _():
            give_parts(0)

        @pl.when(block == per_panel // 8)
        def _():
            give_sums(0)

        @pl.when(block == per_panel // 4 - 1)
        def _():
            solve(0)

        @pl.when(jnp.logical_and(block >= 0, block < per_panel))
        def _():
            panel = reflectors(1, block)
            own[piece(block), :] = panel
            panel_copy(block).start()
            add(1, 0, width, dot(panel, panel, 0, 0))

        @pl.when(jnp.logical_and(block >= per_panel // 4, block < per_panel // 2))
        def _():
            @pl.loop(0, 4)
            def _(more):
                other = (block - per_panel // 4) * 4 + more
                at = piece(other)
                current[:, at] = current[:, at] - dot(solved[0], reflectors(0, other), 1, 1)
                held_copy(other).start()

        @pl.when(jnp.logical_and(block >= per_panel // 2, block < per_panel))
        def _():
            for more in range(2):
                add_inner(1, (block - per_panel // 2) * 2 + more)

    give_parts(1)
    give_sums(1)
    solve(1)

    solved_copy = pltpu.make_async_copy(solved.at[1], solved_ref, solved_sem)
    solved_copy.start()

    @pl.loop(0, total)
    def _(index):
        @pl.when(col < col_n - 1)
        def _():
            to_right(index).wait_send()

        @pl.when(col > 0)
        def _():
            to_left(index).wait_send()

    for step in range(1, row_n):
        if exchange:
            swap(step).wait_send()
        for panel in range(PANELS):
            part_copy(panel, step).wait_send()
            full_copy(panel, step).wait_send()

    @pl.loop(0, per_panel)
    def _(block):
        held_copy(block).wait()
        panel_copy(block).wait()

    solved_copy.wait()


def update_kernel(held_ref, panel_ref, solved_ref, out_ref):
    out_ref[...] = held_ref[...] - dot_split(solved_ref[...], panel_ref[...], 1, 1)


def on_device(row_n, col_n, eigen_rows, householder, owners):
    row_count, width = householder.shape
    give = eigen_rows.shape[0]
    mine_rows = give * row_n
    exchange = give % 8 == 0
    if not exchange:
        eigen_rows = lax.all_to_all(eigen_rows, "row", split_axis=1, concat_axis=0, tiled=True)
    chunk = min(256, row_count)
    per_panel = row_count // chunk
    total = PANELS * per_panel
    col = lax.axis_index("col")
    order = owners[::-1]
    flags = jnp.concatenate([order == col, order <= col]).astype(jnp.int32)
    flags = jnp.broadcast_to(
        jnp.pad(flags, (0, 8 - 2 * PANELS))[:, None], (8, width))
    rows = width + mine_rows
    share = -(-rows // (8 * row_n)) * 8
    dma = pltpu.SemaphoreType.DMA
    held, panel, solved = pl.pallas_call(
        functools.partial(kernel, row_n, col_n, chunk, exchange),
        out_shape=[
            jax.ShapeDtypeStruct((mine_rows, row_count), jnp.float32),
            jax.ShapeDtypeStruct((row_count, width), jnp.float32),
            jax.ShapeDtypeStruct((mine_rows, width), jnp.float32),
        ],
        in_specs=[
            pl.BlockSpec(memory_space=pl.ANY),
            pl.BlockSpec(memory_space=pl.ANY),
            pl.BlockSpec(memory_space=pltpu.VMEM),
        ],
        out_specs=[pl.BlockSpec(memory_space=pl.ANY)] * 3,
        scratch_shapes=[
            pltpu.VMEM((PANELS * row_count, width), jnp.float32),
            pltpu.VMEM((PANELS * row_count, width), jnp.float32),
            pltpu.VMEM((row_count, width), jnp.float32),
            pltpu.VMEM((mine_rows, row_count), jnp.float32),
            pltpu.VMEM((PANELS, share * row_n, width), jnp.float32),
            pltpu.VMEM((PANELS, row_n, share, width), jnp.float32),
            pltpu.VMEM((PANELS, share * row_n, width), jnp.float32),
            pltpu.VMEM((PANELS, mine_rows, width), jnp.float32),
            dma((total,)), dma((total,)), dma((total,)), dma((total,)),
            dma((row_n,)), dma((row_n,)),
            dma((PANELS, row_n)), dma((PANELS, row_n)),
            dma((PANELS, row_n)), dma((PANELS, row_n)),
            dma, dma, dma((per_panel,)), dma((per_panel,)), dma,
        ],
        compiler_params=pltpu.CompilerParams(
            collective_id=0, has_side_effects=True, vmem_limit_bytes=60 * 2**20),
    )(eigen_rows, householder, flags)
    tile = min(1024, row_count)
    return pl.pallas_call(
        update_kernel,
        out_shape=jax.ShapeDtypeStruct((mine_rows, row_count), jnp.float32),
        grid=(row_count // tile,),
        in_specs=[
            pl.BlockSpec((mine_rows, tile), lambda i: (0, i)),
            pl.BlockSpec((tile, width), lambda i: (i, 0)),
            pl.BlockSpec((mine_rows, width), lambda i: (0, 0)),
        ],
        out_specs=pl.BlockSpec((mine_rows, tile), lambda i: (0, i)),
        compiler_params=pltpu.CompilerParams(vmem_limit_bytes=32 * 2**20),
    )(held, panel, solved)


def solution(mesh):
    return jax.shard_map(
        functools.partial(on_device, mesh.shape["row"], mesh.shape["col"]),
        mesh=mesh,
        in_specs=(P(("col", "row"), None), P("row", "col"), P()),
        out_specs=P("col", "row"),
        check_vma=False,
    )
```
